32 devices in a mesh: own: 8 (over z, y), red: 4 (over x, core).
Axes of the slice: x: 2, y: 2, z: 4, core: 2. Of those that a mesh axis runs over, the one named last changes fastest.
Arguments:
- amp_tiles: bfloat16 [2048, 128, 128], P(('own', 'red')), may hold values from -6 to 6
- int_tiles: bfloat16 [2048, 128, 128], P(('own', 'red')), may hold values from -0.0625 to 0.0625
- requests: int32 [8, 4, 8, 2, 8], P('own', 'red'), may hold values from -1 to 63, as said below
- tri_amp: int32 [256, 4, 64], P('own', 'red'), may hold values from 0 to 63, as said below
- tri_int: int32 [256, 4, 64], P('own', 'red'), may hold values from 0 to 63, as said below
- tri_count: int32 [256, 4], P('own', 'red'), may hold values from 1 to 64, as said below
Outputs:
- residual: float32 [256, 128, 128], P(('own', 'red'))
The draws below stay inside these ranges and needn't reach their ends.
Inputs may be any that keep to these rules, and one draw needn't show every extreme that they name: -1 marks an empty slot and live slots come first; the live numbers in one row of 8 slots are distinct; every owner device has 8 live amplitude requests to some holder and 8 live integral requests to some holder. tri_amp[t, r, k] // 8 is a holder h and tri_amp[t, r, k] % 8 is below the number of live amplitude requests of the owner of t, on red index r, to h. `tri_int`: likewise for the integral requests. `tri_count`: on every owner and red index some residual tile has 64 live triples.
All inputs are finite; a program needn't handle non-finite values.
Results may differ from the reference program's by a relative error of at most 0.0003.
Values may be sent and summed in bfloat16 or wider, within the bound.
A program may use at most 128 MiB of HBM per device.

```python
import math
import jax
import jax.numpy as jnp
from jax import lax

TILE = 128
OUT_TILES = 32
SLOTS = 64
CAP = 8
STORE = 64
STORED = 2048
N_OWN = 8
N_RED = 4


def request_plan(key):
    key_count = jax.random.fold_in(key, 11)
    key_full = jax.random.fold_in(key, 12)
    key_perm = jax.random.fold_in(key, 13)
    live_counts = jax.random.randint(key_count, (N_OWN, N_RED, N_OWN, 2), 2, CAP + 1)
    full_holder = jax.random.randint(key_full, (N_OWN, N_RED, 1, 2), 0, N_OWN)
    holder_iota = jnp.arange(N_OWN, dtype=jnp.int32)[None, None, :, None]
    live_counts = jnp.where((holder_iota == full_holder) | (holder_iota == N_OWN - 1), CAP, live_counts)
    perm_keys = jax.random.split(key_perm, N_OWN * N_RED * N_OWN * 2)
    chosen = jax.vmap(lambda single: jax.random.permutation(single, STORE)[:CAP])(perm_keys)
    chosen = chosen.reshape(N_OWN, N_RED, N_OWN, 2, CAP)
    slot_iota = jnp.arange(CAP, dtype=jnp.int32)
    wanted = jnp.where(slot_iota < live_counts[..., None], chosen, -1)
    return (wanted.astype(jnp.int32), live_counts)


def pick_positions(key, live_counts):
    holder = jax.random.randint(jax.random.fold_in(key, 1), (N_OWN, OUT_TILES, N_RED, SLOTS), 0, N_OWN)
    table = jnp.broadcast_to(live_counts[:, None, :, :], (N_OWN, OUT_TILES, N_RED, N_OWN))
    limit = jnp.take_along_axis(table, holder, axis=3)
    slot_pick = jax.random.randint(jax.random.fold_in(key, 2), holder.shape, 0, limit)
    values = holder * CAP + slot_pick
    values = values.at[0, 0, 0, 0].set(N_OWN * CAP - 1)
    values = values.at[0, 0, 0, 1].set(0)
    return values.reshape(N_OWN * OUT_TILES, N_RED, SLOTS).astype(jnp.int32)


def draw_requests(key, part):
    return request_plan(key)[0]


def draw_tri_amp(key, part):
    live_counts = request_plan(key)[1]
    return pick_positions(jax.random.fold_in(key, 21), live_counts[..., 0])


def draw_tri_int(key, part):
    live_counts = request_plan(key)[1]
    return pick_positions(jax.random.fold_in(key, 22), live_counts[..., 1])


def draw_tri_count(key, part):
    factor = jax.random.randint(jax.random.fold_in(key, 31), (N_OWN, 1, N_RED), 1, 5)
    base_count = jax.random.randint(jax.random.fold_in(key, 32), (N_OWN, OUT_TILES, N_RED), 1, SLOTS // 4 + 1)
    counts = jnp.minimum(base_count * factor, SLOTS)
    full_at = jax.random.randint(jax.random.fold_in(key, 33), (N_OWN, 1, N_RED), 0, OUT_TILES)
    tile_iota = jnp.arange(OUT_TILES, dtype=jnp.int32)[None, :, None]
    counts = jnp.where(tile_iota == full_at, SLOTS, counts)
    return counts.reshape(N_OWN * OUT_TILES, N_RED).astype(jnp.int32)


def level_of(rng, shape, cuts, low, high):
    factor_of = 1.0
    for dim, shards_of in cuts:
        draws = jax.random.uniform(jax.random.fold_in(jax.random.fold_in(rng, 6), dim), (shards_of,), jnp.float32, low / len(cuts), high / len(cuts))
        factor_of = factor_of * jnp.repeat(jnp.exp(draws), shape[dim] // shards_of).reshape((-1,) + (1,) * (len(shape) - 1 - dim))
    return factor_of


def scatter_about(rng, extent, width, bound, shards=(), kind=jnp.bfloat16):
    level = level_of(rng, extent, shards, -0.22, 0.18) if shards else 1.0
    values = jax.random.normal(rng, extent, jnp.float32) * width * level
    return jnp.minimum(jnp.maximum(values, -bound), bound).astype(kind)


def setup_inputs(seed: int = 0) -> dict:
    key_of = jax.random.split(jax.random.key(seed), 7)
    return {
        "amp_tiles": scatter_about(key_of[0], (STORED, TILE, TILE), 1.0, 6.0, ((0, 32),)),
        "int_tiles": scatter_about(key_of[1], (STORED, TILE, TILE), (TILE * SLOTS) ** -0.5, 0.0625, ((0, 32),)),
        "requests": draw_requests(jax.random.fold_in(key_of[6], 71), 0),
        "tri_amp": draw_tri_amp(jax.random.fold_in(key_of[6], 71), 0),
        "tri_int": draw_tri_int(jax.random.fold_in(key_of[6], 71), 0),
        "tri_count": draw_tri_count(jax.random.fold_in(key_of[6], 71), 0),
    }


def contract_rows(recv_amp, recv_int, amp_pos, int_pos, counts):
    row_count, slot_count = amp_pos.shape
    block_rows = math.gcd(8, row_count)
    keep_mask = jnp.arange(slot_count, dtype=jnp.int32)[None, :] < counts[:, None]

    def one_block(operands):
        block_amp, block_int, block_keep = operands
        left_tiles = jnp.where(block_keep[:, :, None, None], recv_amp[block_amp], 0).astype(jnp.float32)
        right_tiles = recv_int[block_int].astype(jnp.float32)
        return jnp.einsum("nkpc,nkqc->npq", left_tiles, right_tiles, precision=lax.Precision.HIGHEST)

    def in_blocks(values):
        return values.reshape((row_count // block_rows, block_rows) + values.shape[1:])

    product = lax.map(one_block, (in_blocks(amp_pos), in_blocks(int_pos), in_blocks(keep_mask)))
    return product.reshape(row_count, TILE, TILE)


def reference(amp_tiles, int_tiles, requests, tri_amp, tri_int, tri_count):
    store_amp = amp_tiles.reshape(N_OWN, N_RED, STORE, TILE, TILE)
    store_int = int_tiles.reshape(N_OWN, N_RED, STORE, TILE, TILE)
    holders = jnp.arange(N_OWN, dtype=jnp.int32)

    def receive(store, wanted, red_index):
        clipped = jnp.clip(wanted, 0, STORE - 1).astype(jnp.int32)
        picked = store[holders[:, None], red_index, clipped]
        picked = jnp.where((wanted >= 0)[:, :, None, None], picked, 0)
        return picked.reshape(N_OWN * CAP, TILE, TILE)

    def one_owner(owner):
        first_row = (owner * OUT_TILES).astype(jnp.int32)
        amp_rows = lax.dynamic_slice_in_dim(tri_amp, first_row, OUT_TILES, 0)
        int_rows = lax.dynamic_slice_in_dim(tri_int, first_row, OUT_TILES, 0)
        count_rows = lax.dynamic_slice_in_dim(tri_count, first_row, OUT_TILES, 0)

        def one_partner(total_sum, red_index):
            wanted = requests[owner, red_index]
            recv_amp = receive(store_amp, wanted[:, 0], red_index)
            recv_int = receive(store_int, wanted[:, 1], red_index)
            added = contract_rows(recv_amp, recv_int, amp_rows[:, red_index], int_rows[:, red_index], count_rows[:, red_index])
            return total_sum + added, None

        start_sum = jnp.zeros((OUT_TILES, TILE, TILE), jnp.float32)
        total_sum, unused = lax.scan(one_partner, start_sum, jnp.arange(N_RED, dtype=jnp.int32))
        return total_sum

    result = lax.map(one_owner, jnp.arange(N_OWN, dtype=jnp.int32))
    return result.reshape(N_OWN * OUT_TILES, TILE, TILE)
```

```python
import functools

import jax
import jax.numpy as jnp
from jax import lax
from jax.experimental import pallas as pl
from jax.experimental.pallas import tpu as pltpu
from jax.sharding import PartitionSpec as P

MESH = pl.DeviceIdType.MESH
CORES = 2
GROUP = 16


def flip_bits(value, mask):
    bit = 1
    while bit <= mask:
        if mask & bit:
            value = value + (1 - 2 * ((value // bit) % 2)) * bit
        bit *= 2
    return value


def kernel(
    n_own, n_red, cap, rows, slots,
    req_ref, amp_hbm, int_hbm, tri_amp, tri_int,
    out_ref,
    asked_vmem, asked_smem, amp_store, int_store,
    send_amp, send_int, recv_amp, recv_int, part, sib, across,
    req_send, req_recv, local_sem, tile_send, tile_recv,
    sib_send, sib_recv, across_send, across_recv,
):
    store = amp_store.shape[0]
    received = n_own * cap
    n_x = n_red // CORES
    per_dev = rows // n_red
    me = lax.axis_index("own")
    red = lax.axis_index("red")
    my_x, my_core = red // CORES, red % CORES
    sibling = my_x * CORES + (1 - my_core)

    load_amp = pltpu.make_async_copy(amp_hbm, amp_store, local_sem.at[0])
    load_int = pltpu.make_async_copy(int_hbm, int_store, local_sem.at[1])
    load_amp.start()
    load_int.start()

    barrier = pltpu.get_barrier_semaphore()
    for step in range(1, n_own):
        pl.semaphore_signal(
            barrier, inc=1, device_id={"own": flip_bits(me, step)}, device_id_type=MESH
        )
    pl.semaphore_signal(barrier, inc=1, device_id={"red": sibling}, device_id_type=MESH)
    for step in range(1, n_x):
        peer = ((my_x + step) % n_x) * CORES + my_core
        pl.semaphore_signal(barrier, inc=1, device_id={"red": peer}, device_id_type=MESH)
    pl.semaphore_wait(barrier, n_own - 1 + 1 + n_x - 1)

    steps = sorted(range(1, n_own), reverse=True)

    asks = []
    for step in steps:
        peer = flip_bits(me, step)
        copy = pltpu.make_async_remote_copy(
            src_ref=req_ref.at[peer],
            dst_ref=asked_vmem.at[me],
            send_sem=req_send.at[step],
            recv_sem=req_recv.at[step],
            device_id={"own": peer},
            device_id_type=MESH,
        )
        copy.start()
        asks.append(copy)
    asked_vmem[me] = req_ref[me]
    for copy in asks:
        copy.wait()
    to_smem = pltpu.make_async_copy(asked_vmem, asked_smem, local_sem.at[2])
    to_smem.start()
    to_smem.wait()

    def wanted(peer, kind, slot):
        number = asked_smem[peer, 0, kind * cap + slot]
        return jnp.clip(number, 0, store - 1)

    sends = []
    recv_amp[received] = jnp.zeros_like(recv_amp[received])
    for kind in range(2):
        if kind == 0:
            load_amp.wait()
        else:
            load_int.wait()
        source = (amp_store, int_store)[kind]
        outbox = (send_amp, send_int)[kind]
        inbox = (recv_amp, recv_int)[kind]
        for step in steps + [0]:
            peer = flip_bits(me, step)
            for slot in range(cap):
                tile = source[wanted(peer, kind, slot)]
                if kind == 1:
                    tile = tile.T
                if step == 0:
                    inbox[me * cap + slot] = tile
                else:
                    outbox[step, slot] = tile
            if step == 0:
                continue
            copy = pltpu.make_async_remote_copy(
                src_ref=outbox.at[step],
                dst_ref=inbox.at[pl.ds(me * cap, cap)],
                send_sem=tile_send.at[kind, step],
                recv_sem=tile_recv.at[kind, step],
                device_id={"own": peer},
                device_id_type=MESH,
            )
            copy.start()
            sends.append(copy)
    for copy in sends:
        copy.wait()

    def contract(row):
        def some(block, total):
            first = row * slots + block * GROUP
            left = jnp.concatenate(
                [recv_amp[tri_amp[first + k]] for k in range(GROUP)], axis=1
            )
            right = jnp.concatenate(
                [recv_int[tri_int[first + k]] for k in range(GROUP)], axis=0
            )
            return total + jnp.dot(left, right, preferred_element_type=jnp.float32)

        zero = jnp.zeros(part.shape[1:], jnp.float32)
        return lax.fori_loop(0, slots // GROUP, some, zero)

    def to_sibling(x, j):
        row = (x * CORES + (1 - my_core)) * per_dev + j
        return pltpu.make_async_remote_copy(
            src_ref=part.at[row],
            dst_ref=sib.at[x, j],
            send_sem=sib_send.at[x, j],
            recv_sem=sib_recv.at[x, j],
            device_id={"red": sibling},
            device_id_type=MESH,
        )

    def to_across(step, j):
        x = (my_x + step) % n_x
        row = (x * CORES + my_core) * per_dev + j
        return pltpu.make_async_remote_copy(
            src_ref=part.at[row],
            dst_ref=across.at[step - 1, j],
            send_sem=across_send.at[step - 1, j],
            recv_sem=across_recv.at[step - 1, j],
            device_id={"red": x * CORES + my_core},
            device_id_type=MESH,
        )

    for step in list(range(1, n_x)) + [0]:
        x = (my_x + step) % n_x

        def for_sibling(j, carry):
            row = (x * CORES + (1 - my_core)) * per_dev + j
            part[row] = contract(row)
            to_sibling(x, j).start()
            return carry

        lax.fori_loop(0, per_dev, for_sibling, 0)

        def for_mine(j, carry):
            row = (x * CORES + my_core) * per_dev + j
            value = contract(row)
            to_sibling(x, j).wait_recv()
            if step == 0:
                out_ref[j] = value + sib[x, j]
            else:
                part[row] = value + sib[x, j]
                to_across(step, j).start()
            return carry

        lax.fori_loop(0, per_dev, for_mine, 0)

    for step in range(1, n_x):
        def finish(j, carry):
            to_across(step, j).wait_recv()
            out_ref[j] += across[step - 1, j]
            to_across(step, j).wait_send()
            return carry

        lax.fori_loop(0, per_dev, finish, 0)
    for x in range(n_x):
        def drain(j, carry):
            to_sibling(x, j).wait_send()
            return carry

        lax.fori_loop(0, per_dev, drain, 0)


def body(n_own, n_red, amp_tiles, int_tiles, requests, tri_amp, tri_int, tri_count):
    rows, _, slots = tri_amp.shape
    cap = requests.shape[-1]
    tile = amp_tiles.shape[1:]
    store = amp_tiles.shape[0]
    received = n_own * cap
    n_x = n_red // CORES
    per_dev = rows // n_red
    wide = 128
    asked = requests[0, 0].reshape(n_own, 1, 2 * cap)
    asked = jnp.pad(asked, ((0, 0), (0, 0), (0, wide - 2 * cap)))
    live = lax.broadcasted_iota(jnp.int32, (rows, slots), 1) < tri_count
    left_at = jnp.where(live, tri_amp[:, 0], received).reshape(rows * slots)
    right_at = tri_int[:, 0].reshape(rows * slots)
    vmem = pl.BlockSpec(memory_space=pltpu.VMEM)
    smem = pl.BlockSpec(memory_space=pltpu.SMEM)
    hbm = pl.BlockSpec(memory_space=pl.ANY)
    dma = pltpu.SemaphoreType.DMA
    kind = amp_tiles.dtype
    return pl.pallas_call(
        functools.partial(kernel, n_own, n_red, cap, rows, slots),
        out_shape=jax.ShapeDtypeStruct((per_dev,) + tile, jnp.float32),
        in_specs=[vmem, hbm, hbm, smem, smem],
        out_specs=vmem,
        scratch_shapes=[
            pltpu.VMEM((n_own, 1, wide), jnp.int32),
            pltpu.SMEM((n_own, 1, wide), jnp.int32),
            pltpu.VMEM((store,) + tile, kind),
            pltpu.VMEM((store,) + tile, kind),
            pltpu.VMEM((n_own, cap) + tile, kind),
            pltpu.VMEM((n_own, cap) + tile, kind),
            pltpu.VMEM((received + 1,) + tile, kind),
            pltpu.VMEM((received,) + tile, kind),
            pltpu.VMEM((rows,) + tile, jnp.float32),
            pltpu.VMEM((n_x, per_dev) + tile, jnp.float32),
            pltpu.VMEM((n_x - 1, per_dev) + tile, jnp.float32),
            dma((n_own,)),
            dma((n_own,)),
            dma((3,)),
            dma((2, n_own)),
            dma((2, n_own)),
            dma((n_x, per_dev)),
            dma((n_x, per_dev)),
            dma((n_x - 1, per_dev)),
            dma((n_x - 1, per_dev)),
        ],
        compiler_params=pltpu.CompilerParams(
            collective_id=0, has_side_effects=True, vmem_limit_bytes=40 * 2**20
        ),
        cost_estimate=pl.CostEstimate(
            flops=2 * rows * slots * tile[0] ** 3,
            bytes_accessed=4 * store * tile[0] * tile[1],
            transcendentals=0,
        ),
    )(asked, amp_tiles, int_tiles, left_at, right_at)


def solution(mesh):
    placed = (
        P(("own", "red"), None, None),
        P(("own", "red"), None, None),
        P("own", "red", None, None, None),
        P("own", "red", None),
        P("own", "red", None),
        P("own", "red"),
    )
    return jax.shard_map(
        functools.partial(body, mesh.shape["own"], mesh.shape["red"]),
        mesh=mesh,
        in_specs=placed,
        out_specs=P(("own", "red"), None, None),
        check_vma=False,
    )
```

```python
import functools

import jax
import jax.numpy as jnp
from jax import lax
from jax.experimental import pallas as pl
from jax.experimental.pallas import tpu as pltpu
from jax.sharding import PartitionSpec as P

MESH = pl.DeviceIdType.MESH
CORES = 2
EARLY_GROUP = 32
LATE_GROUP = 8


def flip_bits(value, mask):
    bit = 1
    while bit <= mask:
        if mask & bit:
            value = value + (1 - 2 * ((value // bit) % 2)) * bit
        bit *= 2
    return value


def product(amp_list, int_list):
    left = jnp.concatenate(amp_list, axis=1)
    right = jnp.concatenate(int_list, axis=0)
    return jnp.dot(left, right, preferred_element_type=jnp.float32)


def exchange_kernel(
    n_own, cap, rows, slots,
    req_ref, amp_hbm, int_hbm, tri_amp, tri_int, counts, amp_vec, int_vec,
    recv_amp, far_int, part, late,
    near_int, asked_vmem, asked_smem, amp_store, int_store, send_amp, send_int,
    req_send, req_recv, local_sem, tile_send, tile_recv,
):
    store = amp_store.shape[0]
    received = n_own * cap
    half_own = n_own // 2
    half_slots = half_own * cap
    me = lax.axis_index("own")
    my_half = me // half_own

    load_amp = pltpu.make_async_copy(amp_hbm, amp_store, local_sem.at[0])
    load_int = pltpu.make_async_copy(int_hbm, int_store, local_sem.at[1])
    load_amp.start()
    load_int.start()

    barrier = pltpu.get_barrier_semaphore()
    for step in range(1, n_own):
        pl.semaphore_signal(
            barrier, inc=1, device_id={"own": flip_bits(me, step)}, device_id_type=MESH
        )
    pl.semaphore_wait(barrier, n_own - 1)

    asks = []
    for step in range(n_own - 1, 0, -1):
        peer = flip_bits(me, step)
        copy = pltpu.make_async_remote_copy(
            src_ref=req_ref.at[peer],
            dst_ref=asked_vmem.at[me],
            send_sem=req_send.at[step],
            recv_sem=req_recv.at[step],
            device_id={"own": peer},
            device_id_type=MESH,
        )
        copy.start()
        asks.append(copy)
    asked_vmem[me] = req_ref[me]
    for copy in asks:
        copy.wait()
    to_smem = pltpu.make_async_copy(asked_vmem, asked_smem, local_sem.at[2])
    to_smem.start()
    to_smem.wait()

    far = list(range(n_own - 1, half_own - 1, -1))
    near = list(range(half_own - 1, 0, -1))
    order = []
    for index, step in enumerate(far):
        order.append((0, step))
        if index < len(near):
            order.append((0, near[index]))
    for index, step in enumerate(far):
        if index < len(near):
            order.append((1, near[index]))
        order.append((1, step))

    def pack(kind, step, slot):
        peer = flip_bits(me, step)
        number = asked_smem[peer, kind, slot]
        source = (amp_store, int_store)[kind]
        tile = source[jnp.clip(number, 0, store - 1)]
        return tile.T if kind == 1 else tile

    my_place = (me % half_own) * cap
    recv_amp[received] = jnp.zeros_like(recv_amp[received])
    loaded = [False, False]
    copies = {}
    for kind, step in order:
        if not loaded[kind]:
            (load_amp, load_int)[kind].wait()
            loaded[kind] = True
        outbox = (send_amp, send_int)[kind]
        for slot in range(cap):
            outbox[step, slot] = pack(kind, step, slot)
        if kind == 0:
            inbox = recv_amp.at[pl.ds(me * cap, cap)]
        elif step >= half_own:
            inbox = far_int.at[pl.ds(my_place, cap)]
        else:
            inbox = near_int.at[pl.ds(my_place, cap)]
        copy = pltpu.make_async_remote_copy(
            src_ref=outbox.at[step],
            dst_ref=inbox,
            send_sem=tile_send.at[kind, step],
            recv_sem=tile_recv.at[kind, step],
            device_id={"own": flip_bits(me, step)},
            device_id_type=MESH,
        )
        copy.start()
        copies[kind, step] = copy
    for slot in range(cap):
        recv_amp[me * cap + slot] = pack(0, 0, slot)
        near_int[my_place + slot] = pack(1, 0, slot)

    wide = late.shape[-1]
    row_at = lax.broadcasted_iota(jnp.int32, (rows, slots), 0)
    slot_at = lax.broadcasted_iota(jnp.int32, (rows, slots), 1)
    live = jnp.zeros((rows, slots), jnp.int32)
    for row in range(rows):
        live = jnp.where(row_at == row, counts[row], live)
    amp_at = amp_vec[:, 0, :]
    int_at = int_vec[:, 0, :]
    is_late = (slot_at < live) & ((int_at // half_slots) != my_half)
    late_one = jnp.where(is_late, 1.0, 0.0).astype(jnp.float32)
    before = jnp.where(
        lax.broadcasted_iota(jnp.int32, (slots, slots), 0)
        < lax.broadcasted_iota(jnp.int32, (slots, slots), 1),
        1.0, 0.0,
    ).astype(jnp.float32)
    rank = jnp.dot(late_one, before, preferred_element_type=jnp.float32).astype(jnp.int32)
    rank = jnp.where(is_late, rank, wide)
    place = lax.broadcasted_iota(jnp.int32, (rows, wide), 1)
    total = jnp.sum(late_one, axis=1, keepdims=True).astype(jnp.int32)
    amp_list = jnp.where(place == slots, total, received)
    int_list = jnp.zeros((rows, wide), jnp.int32)
    int_far = int_at % half_slots
    for k in range(slots):
        here = place == rank[:, k : k + 1]
        amp_list = jnp.where(here, amp_at[:, k : k + 1], amp_list)
        int_list = jnp.where(here, int_far[:, k : k + 1], int_list)
    late[0] = amp_list
    late[1] = int_list

    for kind, step in order:
        if kind == 0 or step < half_own:
            copies[kind, step].wait_recv()

    def one_row(row, carry):
        count = counts[row]

        def some(block, total):
            amps, ints = [], []
            for k in range(EARLY_GROUP):
                slot = block * EARLY_GROUP + k
                at = tri_int[row, 0, slot]
                early = ((at // half_slots) == my_half) & (slot < count)
                amps.append(recv_amp[jnp.where(early, tri_amp[row, 0, slot], received)])
                ints.append(near_int[at % half_slots])
            return total + product(amps, ints)

        zero = jnp.zeros(part.shape[1:], jnp.float32)
        part[row] = lax.fori_loop(0, slots // EARLY_GROUP, some, zero)
        return carry

    lax.fori_loop(0, rows, one_row, 0)

    for kind, step in order:
        if kind == 1 and step >= half_own:
            copies[kind, step].wait_recv()
    for kind, step in order:
        copies[kind, step].wait_send()


def late_kernel(rows, slots, late, recv_amp, far_int, part, out):
    def one_row(row, carry):
        count = late[0, row, slots]

        def some(block, total):
            first = block * LATE_GROUP
            amps = [recv_amp[late[0, row, first + k]] for k in range(LATE_GROUP)]
            ints = [far_int[late[1, row, first + k]] for k in range(LATE_GROUP)]
            return total + product(amps, ints)

        blocks = (count + LATE_GROUP - 1) // LATE_GROUP
        out[row] = lax.fori_loop(0, blocks, some, part[row])
        return carry

    lax.fori_loop(0, rows, one_row, 0)


def scatter_kernel(
    n_red, part, out_ref, mid, sib, across, sib_send, sib_recv, across_send, across_recv
):
    n_x = n_red // CORES
    per_dev = part.shape[0] // n_red
    red = lax.axis_index("red")
    my_x, my_core = red // CORES, red % CORES
    sibling = my_x * CORES + (1 - my_core)

    barrier = pltpu.get_barrier_semaphore()
    pl.semaphore_signal(barrier, inc=1, device_id={"red": sibling}, device_id_type=MESH)
    for step in range(1, n_x):
        peer = ((my_x + step) % n_x) * CORES + my_core
        pl.semaphore_signal(barrier, inc=1, device_id={"red": peer}, device_id_type=MESH)
    pl.semaphore_wait(barrier, n_x)

    def to_sibling(step, j):
        x = (my_x + step) % n_x
        return pltpu.make_async_remote_copy(
            src_ref=part.at[(x * CORES + (1 - my_core)) * per_dev + j],
            dst_ref=sib.at[step, j],
            send_sem=sib_send.at[step, j],
            recv_sem=sib_recv.at[step, j],
            device_id={"red": sibling},
            device_id_type=MESH,
        )

    def to_across(step, j):
        x = (my_x + step) % n_x
        return pltpu.make_async_remote_copy(
            src_ref=mid.at[step - 1, j],
            dst_ref=across.at[step - 1, j],
            send_sem=across_send.at[step - 1, j],
            recv_sem=across_recv.at[step - 1, j],
            device_id={"red": x * CORES + my_core},
            device_id_type=MESH,
        )

    order = list(range(1, n_x)) + [0]
    for step in order:
        for j in range(per_dev):
            to_sibling(step, j).start()
    for step in order:
        x = (my_x + step) % n_x
        for j in range(per_dev):
            to_sibling(step, j).wait_recv()
            value = part[(x * CORES + my_core) * per_dev + j] + sib[step, j]
            if step == 0:
                out_ref[j] = value
            else:
                mid[step - 1, j] = value
                to_across(step, j).start()
    for step in range(1, n_x):
        for j in range(per_dev):
            to_across(step, j).wait_recv()
            out_ref[j] += across[step - 1, j]
    for step in order:
        for j in range(per_dev):
            to_sibling(step, j).wait_send()
            if step:
                to_across(step, j).wait_send()


def body(n_own, n_red, amp_tiles, int_tiles, requests, tri_amp, tri_int, tri_count):
    rows, _, slots = tri_amp.shape
    cap = requests.shape[-1]
    tile = amp_tiles.shape[1:]
    store = amp_tiles.shape[0]
    received = n_own * cap
    n_x = n_red // CORES
    per_dev = rows // n_red
    kind = amp_tiles.dtype
    vmem = pl.BlockSpec(memory_space=pltpu.VMEM)
    smem = pl.BlockSpec(memory_space=pltpu.SMEM)
    hbm = pl.BlockSpec(memory_space=pl.ANY)
    dma = pltpu.SemaphoreType.DMA
    shape = jax.ShapeDtypeStruct
    partial = shape((rows,) + tile, jnp.float32)
    counts = tri_count.reshape(rows)
    recv_amp, far_int, early, late = pl.pallas_call(
        functools.partial(exchange_kernel, n_own, cap, rows, slots),
        out_shape=[
            shape((received + 1,) + tile, kind),
            shape((received // 2,) + tile, kind),
            partial,
            shape((2, rows, 2 * slots), jnp.int32),
        ],
        in_specs=[vmem, hbm, hbm, smem, smem, smem, vmem, vmem],
        out_specs=[vmem] * 4,
        scratch_shapes=[
            pltpu.VMEM((received // 2,) + tile, kind),
            pltpu.VMEM((n_own, 2, cap), jnp.int32),
            pltpu.SMEM((n_own, 2, cap), jnp.int32),
            pltpu.VMEM((store,) + tile, kind),
            pltpu.VMEM((store,) + tile, kind),
            pltpu.VMEM((n_own, cap) + tile, kind),
            pltpu.VMEM((n_own, cap) + tile, kind),
            dma((n_own,)),
            dma((n_own,)),
            dma((3,)),
            dma((2, n_own)),
            dma((2, n_own)),
        ],
        compiler_params=pltpu.CompilerParams(
            collective_id=0, has_side_effects=True, vmem_limit_bytes=40 * 2**20
        ),
    )(requests[0, 0], amp_tiles, int_tiles, tri_amp, tri_int, counts, tri_amp, tri_int)
    summed = pl.pallas_call(
        functools.partial(late_kernel, rows, slots),
        out_shape=partial,
        in_specs=[smem, vmem, vmem, vmem],
        out_specs=vmem,
        compiler_params=pltpu.CompilerParams(vmem_limit_bytes=32 * 2**20),
    )(late, recv_amp, far_int, early)
    return pl.pallas_call(
        functools.partial(scatter_kernel, n_red),
        out_shape=shape((per_dev,) + tile, jnp.float32),
        in_specs=[vmem],
        out_specs=vmem,
        scratch_shapes=[
            pltpu.VMEM((n_x - 1, per_dev) + tile, jnp.float32),
            pltpu.VMEM((n_x, per_dev) + tile, jnp.float32),
            pltpu.VMEM((n_x - 1, per_dev) + tile, jnp.float32),
            dma((n_x, per_dev)),
            dma((n_x, per_dev)),
            dma((n_x - 1, per_dev)),
            dma((n_x - 1, per_dev)),
        ],
        compiler_params=pltpu.CompilerParams(
            collective_id=1, has_side_effects=True, vmem_limit_bytes=32 * 2**20
        ),
    )(summed)


def solution(mesh):
    placed = (
        P(("own", "red"), None, None),
        P(("own", "red"), None, None),
        P("own", "red", None, None, None),
        P("own", "red", None),
        P("own", "red", None),
        P("own", "red"),
    )
    return jax.shard_map(
        functools.partial(body, mesh.shape["own"], mesh.shape["red"]),
        mesh=mesh,
        in_specs=placed,
        out_specs=P(("own", "red"), None, None),
        check_vma=False,
    )
```

```python
import functools

import jax
import jax.numpy as jnp
from jax import lax
from jax.experimental import pallas as pl
from jax.experimental.pallas import tpu as pltpu
from jax.sharding import PartitionSpec as P

MESH = pl.DeviceIdType.MESH
CORES = 2
EARLY_PARTS = 2
GROUP = 8
ITEMS = 4


def flip_bits(value, mask):
    bit = 1
    while bit <= mask:
        if mask & bit:
            value = value + (1 - 2 * ((value // bit) % 2)) * bit
        bit *= 2
    return value


def product(amp_list, int_list):
    left = jnp.concatenate(amp_list, axis=1)
    right = jnp.concatenate(int_list, axis=0)
    return jnp.dot(left, right, preferred_element_type=jnp.float32)


def exchange_kernel(
    n_own, cap, rows, slots,
    req_hbm, amp_hbm, int_hbm, amp_at_hbm, int_at_hbm, count_hbm,
    amp_out, far_int, part, late,
    recv_amp, near_int, req_ref, tri_amp, tri_int, counts, amp_vec, int_vec, asked_vmem, asked_smem, amp_store, int_store, send_amp, send_int,
    req_send, req_recv, local_sem, tile_send, tile_recv,
):
    store = amp_store.shape[0]
    received = n_own * cap
    half_own = n_own // 2
    half_slots = half_own * cap
    me = lax.axis_index("own")
    my_half = me // half_own

    load_amp = pltpu.make_async_copy(amp_hbm, amp_store, local_sem.at[0])
    load_int = pltpu.make_async_copy(int_hbm, int_store, local_sem.at[1])
    load_req = pltpu.make_async_copy(req_hbm, req_ref, local_sem.at[3])
    load_req.start()
    load_amp.start()
    load_int.start()
    loads = []
    for index, (src, dst) in enumerate([
        (amp_at_hbm, tri_amp), (int_at_hbm, tri_int), (count_hbm, counts),
        (amp_at_hbm, amp_vec), (int_at_hbm, int_vec),
    ]):
        load = pltpu.make_async_copy(src, dst, local_sem.at[4 + index])
        load.start()
        loads.append(load)

    barrier = pltpu.get_barrier_semaphore()
    for step in range(1, n_own):
        pl.semaphore_signal(
            barrier, inc=1, device_id={"own": flip_bits(me, step)}, device_id_type=MESH
        )
    pl.semaphore_wait(barrier, n_own - 1)

    load_req.wait()
    asks = []
    for step in range(n_own - 1, 0, -1):
        peer = flip_bits(me, step)
        copy = pltpu.make_async_remote_copy(
            src_ref=req_ref.at[peer],
            dst_ref=asked_vmem.at[me],
            send_sem=req_send.at[step],
            recv_sem=req_recv.at[step],
            device_id={"own": peer},
            device_id_type=MESH,
        )
        copy.start()
        asks.append(copy)
    asked_vmem[me] = req_ref[me]
    for copy in asks:
        copy.wait()
    to_smem = pltpu.make_async_copy(asked_vmem, asked_smem, local_sem.at[2])
    to_smem.start()
    to_smem.wait()

    far = list(range(n_own - 1, half_own - 1, -1))
    near = list(range(half_own - 1, 0, -1))
    order = []
    for index, step in enumerate(far):
        order.append((0, step))
        if index < len(near):
            order.append((0, near[index]))
    for index, step in enumerate(far):
        if index < len(near):
            order.append((1, near[index]))
        order.append((1, step))

    def pack(kind, step, slot):
        peer = flip_bits(me, step)
        number = asked_smem[peer, kind, slot]
        source = (amp_store, int_store)[kind]
        tile = source[jnp.clip(number, 0, store - 1)]
        return tile.T if kind == 1 else tile

    my_place = (me % half_own) * cap
    recv_amp[received] = jnp.zeros_like(recv_amp[received])
    loaded = [False, False]
    copies = {}
    for kind, step in order:
        if not loaded[kind]:
            (load_amp, load_int)[kind].wait()
            loaded[kind] = True
        outbox = (send_amp, send_int)[kind]
        for slot in range(cap):
            outbox[step, slot] = pack(kind, step, slot)
        if kind == 0:
            inbox = recv_amp.at[pl.ds(me * cap, cap)]
        elif step >= half_own:
            inbox = far_int.at[pl.ds(my_place, cap)]
        else:
            inbox = near_int.at[pl.ds(my_place, cap)]
        copy = pltpu.make_async_remote_copy(
            src_ref=outbox.at[step],
            dst_ref=inbox,
            send_sem=tile_send.at[kind, step],
            recv_sem=tile_recv.at[kind, step],
            device_id={"own": flip_bits(me, step)},
            device_id_type=MESH,
        )
        copy.start()
        copies[kind, step] = copy
    for slot in range(cap):
        recv_amp[me * cap + slot] = pack(0, 0, slot)
        near_int[my_place + slot] = pack(1, 0, slot)

    for load in loads:
        load.wait()

    wide = late.shape[-1]
    row_at = lax.broadcasted_iota(jnp.int32, (rows, slots), 0)
    slot_at = lax.broadcasted_iota(jnp.int32, (rows, slots), 1)
    live = jnp.zeros((rows, slots), jnp.int32)
    for row in range(rows):
        live = jnp.where(row_at == row, counts[row], live)
    amp_at = amp_vec[:, 0, :]
    int_at = int_vec[:, 0, :]
    is_late = (slot_at < live) & ((int_at // half_slots) != my_half)
    late_one = jnp.where(is_late, 1.0, 0.0).astype(jnp.float32)
    before = jnp.where(
        lax.broadcasted_iota(jnp.int32, (slots, slots), 0)
        < lax.broadcasted_iota(jnp.int32, (slots, slots), 1),
        1.0, 0.0,
    ).astype(jnp.float32)
    rank = jnp.dot(late_one, before, preferred_element_type=jnp.float32).astype(jnp.int32)
    rank = jnp.where(is_late, rank, wide)
    place = lax.broadcasted_iota(jnp.int32, (rows, wide), 1)
    total = jnp.sum(late_one, axis=1, keepdims=True).astype(jnp.int32)
    amp_list = jnp.where(place == slots, total, received)
    int_list = jnp.zeros((rows, wide), jnp.int32)
    int_far = int_at % half_slots
    for k in range(slots):
        here = place == rank[:, k : k + 1]
        amp_list = jnp.where(here, amp_at[:, k : k + 1], amp_list)
        int_list = jnp.where(here, int_far[:, k : k + 1], int_list)
    late[0] = amp_list
    late[1] = int_list

    blocks = ((total + (GROUP - 1)) // GROUP).astype(jnp.float32)
    lower = jnp.where(
        lax.broadcasted_iota(jnp.int32, (rows, rows), 1)
        < lax.broadcasted_iota(jnp.int32, (rows, rows), 0),
        1.0, 0.0,
    ).astype(jnp.float32)
    ahead = jnp.dot(
        lower, jnp.broadcast_to(blocks, (rows, wide)), preferred_element_type=jnp.float32
    ).astype(jnp.int32)
    item_count = jnp.sum(blocks).astype(jnp.int32)
    item_rows = rows * slots // GROUP // wide
    for line in range(item_rows):
        item = lax.broadcasted_iota(jnp.int32, (rows, wide), 1) + line * wide
        begun = ahead <= item
        row_of = jnp.sum(begun.astype(jnp.int32), axis=0, keepdims=True) - 1
        start = jnp.max(jnp.where(begun, ahead, 0), axis=0, keepdims=True)
        first_of = (item[:1] - start) * GROUP
        listed = item[:1] < item_count
        late[2, line : line + 1] = jnp.where(listed, row_of, 0)
        late[2, item_rows + line : item_rows + line + 1] = jnp.where(
            listed, first_of, slots + GROUP
        )
    late[2, 2 * item_rows : 2 * item_rows + 1] = jnp.broadcast_to(item_count, (1, wide))

    for kind, step in order:
        if kind == 0 or step < half_own:
            copies[kind, step].wait_recv()
    keep_amp = pltpu.make_async_copy(recv_amp, amp_out, local_sem.at[9])
    keep_amp.start()

    def one_row(row, carry):
        count = counts[row]
        total = None
        for piece in range(EARLY_PARTS):
            amps, ints = [], []
            for k in range(slots // EARLY_PARTS):
                slot = piece * (slots // EARLY_PARTS) + k
                at = tri_int[row, 0, slot]
                early = ((at // half_slots) == my_half) & (slot < count)
                amps.append(recv_amp[jnp.where(early, tri_amp[row, 0, slot], received)])
                ints.append(near_int[at % half_slots])
            value = product(amps, ints)
            total = value if total is None else total + value
        part[row] = total
        return carry

    lax.fori_loop(0, rows, one_row, 0)

    for kind, step in order:
        if kind == 1 and step >= half_own:
            copies[kind, step].wait_recv()
    for kind, step in order:
        copies[kind, step].wait_send()
    keep_amp.wait()


def late_kernel(rows, slots, late, recv_amp, far_int, part, out):
    wide = late.shape[-1]
    item_rows = rows * slots // GROUP // wide

    def some(block, carry):
        found = []
        for index in range(ITEMS):
            item = block * ITEMS + index
            line, column = item // wide, item % wide
            row = late[2, line, column]
            first = late[2, item_rows + line, column]
            amps = [recv_amp[late[0, row, first + k]] for k in range(GROUP)]
            ints = [far_int[late[1, row, first + k]] for k in range(GROUP)]
            found.append((row, product(amps, ints)))
        for row, value in found:
            out[row] += value
        return carry

    items = late[2, 2 * item_rows, 0]
    lax.fori_loop(0, (items + ITEMS - 1) // ITEMS, some, 0)


def scatter_kernel(
    n_red, part, out_ref, mid, sib, across, sib_send, sib_recv, across_send, across_recv
):
    n_x = n_red // CORES
    per_dev = part.shape[0] // n_red
    red = lax.axis_index("red")
    my_x, my_core = red // CORES, red % CORES
    sibling = my_x * CORES + (1 - my_core)

    barrier = pltpu.get_barrier_semaphore()
    pl.semaphore_signal(barrier, inc=1, device_id={"red": sibling}, device_id_type=MESH)
    for step in range(1, n_x):
        peer = ((my_x + step) % n_x) * CORES + my_core
        pl.semaphore_signal(barrier, inc=1, device_id={"red": peer}, device_id_type=MESH)
    pl.semaphore_wait(barrier, n_x)

    def to_sibling(step, j):
        x = (my_x + step) % n_x
        return pltpu.make_async_remote_copy(
            src_ref=part.at[(x * CORES + (1 - my_core)) * per_dev + j],
            dst_ref=sib.at[step, j],
            send_sem=sib_send.at[step, j],
            recv_sem=sib_recv.at[step, j],
            device_id={"red": sibling},
            device_id_type=MESH,
        )

    def to_across(step, j):
        x = (my_x + step) % n_x
        return pltpu.make_async_remote_copy(
            src_ref=mid.at[step - 1, j],
            dst_ref=across.at[step - 1, j],
            send_sem=across_send.at[step - 1, j],
            recv_sem=across_recv.at[step - 1, j],
            device_id={"red": x * CORES + my_core},
            device_id_type=MESH,
        )

    order = list(range(1, n_x)) + [0]
    for step in order:
        for j in range(per_dev):
            to_sibling(step, j).start()
    for step in order:
        x = (my_x + step) % n_x
        for j in range(per_dev):
            to_sibling(step, j).wait_recv()
            value = part[(x * CORES + my_core) * per_dev + j] + sib[step, j]
            if step == 0:
                out_ref[j] = value
            else:
                mid[step - 1, j] = value
                to_across(step, j).start()
    for step in range(1, n_x):
        for j in range(per_dev):
            to_across(step, j).wait_recv()
            out_ref[j] += across[step - 1, j]
    for step in order:
        for j in range(per_dev):
            to_sibling(step, j).wait_send()
            if step:
                to_across(step, j).wait_send()


def body(n_own, n_red, amp_tiles, int_tiles, requests, tri_amp, tri_int, tri_count):
    rows, _, slots = tri_amp.shape
    cap = requests.shape[-1]
    tile = amp_tiles.shape[1:]
    store = amp_tiles.shape[0]
    received = n_own * cap
    n_x = n_red // CORES
    per_dev = rows // n_red
    kind = amp_tiles.dtype
    vmem = pl.BlockSpec(memory_space=pltpu.VMEM)
    smem = pl.BlockSpec(memory_space=pltpu.SMEM)
    hbm = pl.BlockSpec(memory_space=pltpu.HBM)
    dma = pltpu.SemaphoreType.DMA
    shape = jax.ShapeDtypeStruct
    partial = shape((rows,) + tile, jnp.float32)
    counts = tri_count.reshape(rows)
    recv_amp, far_int, early, late = pl.pallas_call(
        functools.partial(exchange_kernel, n_own, cap, rows, slots),
        out_shape=[
            shape((received + 1,) + tile, kind),
            shape((received // 2,) + tile, kind),
            partial,
            shape((3, rows, 2 * slots), jnp.int32),
        ],
        in_specs=[hbm] * 6,
        out_specs=[hbm, vmem, vmem, vmem],
        scratch_shapes=[
            pltpu.VMEM((received + 1,) + tile, kind),
            pltpu.VMEM((received // 2,) + tile, kind),
            pltpu.VMEM((n_own, 2, cap), jnp.int32),
            pltpu.SMEM((rows, 1, slots), jnp.int32),
            pltpu.SMEM((rows, 1, slots), jnp.int32),
            pltpu.SMEM((rows,), jnp.int32),
            pltpu.VMEM((rows, 1, slots), jnp.int32),
            pltpu.VMEM((rows, 1, slots), jnp.int32),
            pltpu.VMEM((n_own, 2, cap), jnp.int32),
            pltpu.SMEM((n_own, 2, cap), jnp.int32),
            pltpu.VMEM((store,) + tile, kind),
            pltpu.VMEM((store,) + tile, kind),
            pltpu.VMEM((n_own, cap) + tile, kind),
            pltpu.VMEM((n_own, cap) + tile, kind),
            dma((n_own,)),
            dma((n_own,)),
            dma((10,)),
            dma((2, n_own)),
            dma((2, n_own)),
        ],
        compiler_params=pltpu.CompilerParams(
            collective_id=0, has_side_effects=True, vmem_limit_bytes=50 * 2**20
        ),
    )(requests[0, 0], amp_tiles, int_tiles, tri_amp, tri_int, counts)
    summed = pl.pallas_call(
        functools.partial(late_kernel, rows, slots),
        out_shape=partial,
        in_specs=[smem, vmem, vmem, vmem],
        out_specs=vmem,
        input_output_aliases={3: 0},
        compiler_params=pltpu.CompilerParams(vmem_limit_bytes=32 * 2**20),
    )(late, recv_amp, far_int, early)
    return pl.pallas_call(
        functools.partial(scatter_kernel, n_red),
        out_shape=shape((per_dev,) + tile, jnp.float32),
        in_specs=[vmem],
        out_specs=vmem,
        scratch_shapes=[
            pltpu.VMEM((n_x - 1, per_dev) + tile, jnp.float32),
            pltpu.VMEM((n_x, per_dev) + tile, jnp.float32),
            pltpu.VMEM((n_x - 1, per_dev) + tile, jnp.float32),
            dma((n_x, per_dev)),
            dma((n_x, per_dev)),
            dma((n_x - 1, per_dev)),
            dma((n_x - 1, per_dev)),
        ],
        compiler_params=pltpu.CompilerParams(
            collective_id=1, has_side_effects=True, vmem_limit_bytes=32 * 2**20
        ),
    )(summed)


def solution(mesh):
    placed = (
        P(("own", "red"), None, None),
        P(("own", "red"), None, None),
        P("own", "red", None, None, None),
        P("own", "red", None),
        P("own", "red", None),
        P("own", "red"),
    )
    return jax.shard_map(
        functools.partial(body, mesh.shape["own"], mesh.shape["red"]),
        mesh=mesh,
        in_specs=placed,
        out_specs=P(("own", "red"), None, None),
        check_vma=False,
    )
```

```python
import functools

import jax
import jax.numpy as jnp
from jax import lax
from jax.experimental import pallas as pl
from jax.experimental.pallas import tpu as pltpu
from jax.sharding import PartitionSpec as P

MESH = pl.DeviceIdType.MESH
CORES = 2
EARLY_PARTS = 2
GROUP = 4
ITEMS = 8


def flip_bits(value, mask):
    bit = 1
    while bit <= mask:
        if mask & bit:
            value = value + (1 - 2 * ((value // bit) % 2)) * bit
        bit *= 2
    return value


def product(amp_list, int_list):
    left = jnp.concatenate(amp_list, axis=1)
    right = jnp.concatenate(int_list, axis=0)
    return jnp.dot(left, right, preferred_element_type=jnp.float32)


def exchange_kernel(
    n_own, cap, rows, slots,
    req_hbm, amp_hbm, int_hbm, amp_at_hbm, int_at_hbm, count_hbm,
    amp_out, far_int, part, late,
    recv_amp, near_int, req_ref, tri_amp, tri_int, counts, amp_vec, int_vec, asked_vmem, asked_smem, amp_store, int_store, send_amp, send_int,
    req_send, req_recv, local_sem, tile_send, tile_recv,
):
    store = amp_store.shape[0]
    received = n_own * cap
    half_own = n_own // 2
    half_slots = half_own * cap
    me = lax.axis_index("own")
    my_half = me // half_own

    load_amp = pltpu.make_async_copy(amp_hbm, amp_store, local_sem.at[0])
    load_int = pltpu.make_async_copy(int_hbm, int_store, local_sem.at[1])
    load_req = pltpu.make_async_copy(req_hbm, req_ref, local_sem.at[3])
    load_req.start()
    load_amp.start()
    load_int.start()
    loads = []
    for index, (src, dst) in enumerate([
        (amp_at_hbm, tri_amp), (int_at_hbm, tri_int), (count_hbm, counts),
        (amp_at_hbm, amp_vec), (int_at_hbm, int_vec),
    ]):
        load = pltpu.make_async_copy(src, dst, local_sem.at[4 + index])
        load.start()
        loads.append(load)

    barrier = pltpu.get_barrier_semaphore()
    for step in range(1, n_own):
        pl.semaphore_signal(
            barrier, inc=1, device_id={"own": flip_bits(me, step)}, device_id_type=MESH
        )
    pl.semaphore_wait(barrier, n_own - 1)

    load_req.wait()
    asks = []
    for step in range(n_own - 1, 0, -1):
        peer = flip_bits(me, step)
        copy = pltpu.make_async_remote_copy(
            src_ref=req_ref.at[peer],
            dst_ref=asked_vmem.at[me],
            send_sem=req_send.at[step],
            recv_sem=req_recv.at[step],
            device_id={"own": peer},
            device_id_type=MESH,
        )
        copy.start()
        asks.append(copy)
    asked_vmem[me] = req_ref[me]
    for copy in asks:
        copy.wait()
    to_smem = pltpu.make_async_copy(asked_vmem, asked_smem, local_sem.at[2])
    to_smem.start()
    to_smem.wait()

    far = list(range(n_own - 1, half_own - 1, -1))
    near = list(range(half_own - 1, 0, -1))
    near_work = [(0, step) for step in near] + [(1, step) for step in near]
    order = []
    for index, step in enumerate(far):
        order.append((0, step))
        share = -(-len(near_work) // (len(far) - index))
        order += near_work[:share]
        near_work = near_work[share:]
    order += [(1, step) for step in far]
    first_far = far[0]
    first_holder = n_own - 1 - me

    def pack(kind, step, slot):
        peer = flip_bits(me, step)
        number = asked_smem[peer, kind, slot]
        source = (amp_store, int_store)[kind]
        tile = source[jnp.clip(number, 0, store - 1)]
        return tile.T if kind == 1 else tile

    my_place = (me % half_own) * cap
    recv_amp[received] = jnp.zeros_like(recv_amp[received])
    loaded = [False, False]
    copies = {}
    for kind, step in order:
        if not loaded[kind]:
            (load_amp, load_int)[kind].wait()
            loaded[kind] = True
        outbox = (send_amp, send_int)[kind]
        for slot in range(cap):
            outbox[step, slot] = pack(kind, step, slot)
        if kind == 0:
            inbox = recv_amp.at[pl.ds(me * cap, cap)]
        elif step == first_far:
            inbox = near_int.at[pl.ds(half_slots, cap)]
        elif step >= half_own:
            inbox = far_int.at[pl.ds(my_place, cap)]
        else:
            inbox = near_int.at[pl.ds(my_place, cap)]
        copy = pltpu.make_async_remote_copy(
            src_ref=outbox.at[step],
            dst_ref=inbox,
            send_sem=tile_send.at[kind, step],
            recv_sem=tile_recv.at[kind, step],
            device_id={"own": flip_bits(me, step)},
            device_id_type=MESH,
        )
        copy.start()
        copies[kind, step] = copy
    for slot in range(cap):
        recv_amp[me * cap + slot] = pack(0, 0, slot)
        near_int[my_place + slot] = pack(1, 0, slot)

    for load in loads:
        load.wait()

    wide = late.shape[-1]
    row_at = lax.broadcasted_iota(jnp.int32, (rows, slots), 0)
    slot_at = lax.broadcasted_iota(jnp.int32, (rows, slots), 1)
    live = jnp.zeros((rows, slots), jnp.int32)
    for row in range(rows):
        live = jnp.where(row_at == row, counts[row], live)
    amp_at = amp_vec[:, 0, :]
    int_at = int_vec[:, 0, :]
    is_late = (slot_at < live) & ((int_at // half_slots) != my_half)
    is_late = is_late & ((int_at // cap) != first_holder)
    late_one = jnp.where(is_late, 1.0, 0.0).astype(jnp.float32)
    before = jnp.where(
        lax.broadcasted_iota(jnp.int32, (slots, slots), 0)
        < lax.broadcasted_iota(jnp.int32, (slots, slots), 1),
        1.0, 0.0,
    ).astype(jnp.float32)
    rank = jnp.dot(late_one, before, preferred_element_type=jnp.float32).astype(jnp.int32)
    rank = jnp.where(is_late, rank, wide)
    place = lax.broadcasted_iota(jnp.int32, (rows, wide), 1)
    total = jnp.sum(late_one, axis=1, keepdims=True).astype(jnp.int32)
    amp_list = jnp.where(place == slots, total, received)
    filled = ((first_holder + 1) % half_own) * cap
    int_list = jnp.zeros((rows, wide), jnp.int32) + filled
    int_far = int_at % half_slots
    for k in range(slots):
        here = place == rank[:, k : k + 1]
        amp_list = jnp.where(here, amp_at[:, k : k + 1], amp_list)
        int_list = jnp.where(here, int_far[:, k : k + 1], int_list)
    late[0] = amp_list
    late[1] = int_list

    blocks = ((total + (GROUP - 1)) // GROUP).astype(jnp.float32)
    lower = jnp.where(
        lax.broadcasted_iota(jnp.int32, (rows, rows), 1)
        < lax.broadcasted_iota(jnp.int32, (rows, rows), 0),
        1.0, 0.0,
    ).astype(jnp.float32)
    ahead = jnp.dot(
        lower, jnp.broadcast_to(blocks, (rows, wide)), preferred_element_type=jnp.float32
    ).astype(jnp.int32)
    item_count = jnp.sum(blocks).astype(jnp.int32)
    item_rows = rows * slots // GROUP // wide
    for line in range(item_rows):
        item = lax.broadcasted_iota(jnp.int32, (rows, wide), 1) + line * wide
        begun = ahead <= item
        row_of = jnp.sum(begun.astype(jnp.int32), axis=0, keepdims=True) - 1
        start = jnp.max(jnp.where(begun, ahead, 0), axis=0, keepdims=True)
        first_of = (item[:1] - start) * GROUP
        listed = item[:1] < item_count
        late[2, line : line + 1] = jnp.where(listed, row_of, 0)
        late[2, item_rows + line : item_rows + line + 1] = jnp.where(
            listed, first_of, slots + GROUP
        )
    late[2, 2 * item_rows : 2 * item_rows + 1] = jnp.broadcast_to(item_count, (1, wide))

    for kind, step in order:
        if kind == 0 or step < half_own or step == first_far:
            copies[kind, step].wait_recv()
    keep_amp = pltpu.make_async_copy(recv_amp, amp_out, local_sem.at[9])
    keep_amp.start()

    def one_row(row, carry):
        count = counts[row]
        total = None
        for piece in range(EARLY_PARTS):
            amps, ints = [], []
            for k in range(slots // EARLY_PARTS):
                slot = piece * (slots // EARLY_PARTS) + k
                at = tri_int[row, 0, slot]
                first = (at // cap) == first_holder
                early = (((at // half_slots) == my_half) | first) & (slot < count)
                amps.append(recv_amp[jnp.where(early, tri_amp[row, 0, slot], received)])
                ints.append(near_int[jnp.where(first, half_slots + at % cap, at % half_slots)])
            value = product(amps, ints)
            total = value if total is None else total + value
        part[row] = total
        return carry

    lax.fori_loop(0, rows, one_row, 0)

    for kind, step in order:
        if kind == 1 and half_own <= step < first_far:
            copies[kind, step].wait_recv()
    for kind, step in order:
        copies[kind, step].wait_send()
    keep_amp.wait()


def late_kernel(rows, slots, late, recv_amp, far_int, part, out):
    wide = late.shape[-1]
    item_rows = rows * slots // GROUP // wide

    def some(block, carry):
        found = []
        for index in range(ITEMS):
            item = block * ITEMS + index
            line, column = item // wide, item % wide
            row = late[2, line, column]
            first = late[2, item_rows + line, column]
            amps = [recv_amp[late[0, row, first + k]] for k in range(GROUP)]
            ints = [far_int[late[1, row, first + k]] for k in range(GROUP)]
            found.append((row, product(amps, ints)))
        for row, value in found:
            out[row] += value
        return carry

    items = late[2, 2 * item_rows, 0]
    lax.fori_loop(0, (items + ITEMS - 1) // ITEMS, some, 0)


def scatter_kernel(
    n_red, part, out_ref, mid, sib, across, sib_send, sib_recv, across_send, across_recv
):
    n_x = n_red // CORES
    per_dev = part.shape[0] // n_red
    red = lax.axis_index("red")
    my_x, my_core = red // CORES, red % CORES
    sibling = my_x * CORES + (1 - my_core)

    barrier = pltpu.get_barrier_semaphore()
    pl.semaphore_signal(barrier, inc=1, device_id={"red": sibling}, device_id_type=MESH)
    for step in range(1, n_x):
        peer = ((my_x + step) % n_x) * CORES + my_core
        pl.semaphore_signal(barrier, inc=1, device_id={"red": peer}, device_id_type=MESH)
    pl.semaphore_wait(barrier, n_x)

    def to_sibling(step, j):
        x = (my_x + step) % n_x
        return pltpu.make_async_remote_copy(
            src_ref=part.at[(x * CORES + (1 - my_core)) * per_dev + j],
            dst_ref=sib.at[step, j],
            send_sem=sib_send.at[step, j],
            recv_sem=sib_recv.at[step, j],
            device_id={"red": sibling},
            device_id_type=MESH,
        )

    def to_across(step, j):
        x = (my_x + step) % n_x
        return pltpu.make_async_remote_copy(
            src_ref=mid.at[step - 1, j],
            dst_ref=across.at[step - 1, j],
            send_sem=across_send.at[step - 1, j],
            recv_sem=across_recv.at[step - 1, j],
            device_id={"red": x * CORES + my_core},
            device_id_type=MESH,
        )

    order = list(range(1, n_x)) + [0]
    for step in order:
        for j in range(per_dev):
            to_sibling(step, j).start()
    for step in order:
        x = (my_x + step) % n_x
        for j in range(per_dev):
            to_sibling(step, j).wait_recv()
            value = part[(x * CORES + my_core) * per_dev + j] + sib[step, j]
            if step == 0:
                out_ref[j] = value
            else:
                mid[step - 1, j] = value
                to_across(step, j).start()
    for step in range(1, n_x):
        for j in range(per_dev):
            to_across(step, j).wait_recv()
            out_ref[j] += across[step - 1, j]
    for step in order:
        for j in range(per_dev):
            to_sibling(step, j).wait_send()
            if step:
                to_across(step, j).wait_send()


def body(n_own, n_red, amp_tiles, int_tiles, requests, tri_amp, tri_int, tri_count):
    rows, _, slots = tri_amp.shape
    cap = requests.shape[-1]
    tile = amp_tiles.shape[1:]
    store = amp_tiles.shape[0]
    received = n_own * cap
    n_x = n_red // CORES
    per_dev = rows // n_red
    kind = amp_tiles.dtype
    vmem = pl.BlockSpec(memory_space=pltpu.VMEM)
    smem = pl.BlockSpec(memory_space=pltpu.SMEM)
    hbm = pl.BlockSpec(memory_space=pltpu.HBM)
    dma = pltpu.SemaphoreType.DMA
    shape = jax.ShapeDtypeStruct
    partial = shape((rows,) + tile, jnp.float32)
    counts = tri_count.reshape(rows)
    recv_amp, far_int, early, late = pl.pallas_call(
        functools.partial(exchange_kernel, n_own, cap, rows, slots),
        out_shape=[
            shape((received + 1,) + tile, kind),
            shape((received // 2,) + tile, kind),
            partial,
            shape((3, rows, 2 * slots), jnp.int32),
        ],
        in_specs=[hbm] * 6,
        out_specs=[hbm, vmem, vmem, vmem],
        scratch_shapes=[
            pltpu.VMEM((received + 1,) + tile, kind),
            pltpu.VMEM((received // 2 + cap,) + tile, kind),
            pltpu.VMEM((n_own, 2, cap), jnp.int32),
            pltpu.SMEM((rows, 1, slots), jnp.int32),
            pltpu.SMEM((rows, 1, slots), jnp.int32),
            pltpu.SMEM((rows,), jnp.int32),
            pltpu.VMEM((rows, 1, slots), jnp.int32),
            pltpu.VMEM((rows, 1, slots), jnp.int32),
            pltpu.VMEM((n_own, 2, cap), jnp.int32),
            pltpu.SMEM((n_own, 2, cap), jnp.int32),
            pltpu.VMEM((store,) + tile, kind),
            pltpu.VMEM((store,) + tile, kind),
            pltpu.VMEM((n_own, cap) + tile, kind),
            pltpu.VMEM((n_own, cap) + tile, kind),
            dma((n_own,)),
            dma((n_own,)),
            dma((10,)),
            dma((2, n_own)),
            dma((2, n_own)),
        ],
        compiler_params=pltpu.CompilerParams(
            collective_id=0, has_side_effects=True, vmem_limit_bytes=50 * 2**20
        ),
    )(requests[0, 0], amp_tiles, int_tiles, tri_amp, tri_int, counts)
    summed = pl.pallas_call(
        functools.partial(late_kernel, rows, slots),
        out_shape=partial,
        in_specs=[smem, vmem, vmem, vmem],
        out_specs=vmem,
        input_output_aliases={3: 0},
        compiler_params=pltpu.CompilerParams(vmem_limit_bytes=32 * 2**20),
    )(late, recv_amp, far_int, early)
    return pl.pallas_call(
        functools.partial(scatter_kernel, n_red),
        out_shape=shape((per_dev,) + tile, jnp.float32),
        in_specs=[vmem],
        out_specs=vmem,
        scratch_shapes=[
            pltpu.VMEM((n_x - 1, per_dev) + tile, jnp.float32),
            pltpu.VMEM((n_x, per_dev) + tile, jnp.float32),
            pltpu.VMEM((n_x - 1, per_dev) + tile, jnp.float32),
            dma((n_x, per_dev)),
            dma((n_x, per_dev)),
            dma((n_x - 1, per_dev)),
            dma((n_x - 1, per_dev)),
        ],
        compiler_params=pltpu.CompilerParams(
            collective_id=1, has_side_effects=True, vmem_limit_bytes=32 * 2**20
        ),
    )(summed)


def solution(mesh):
    placed = (
        P(("own", "red"), None, None),
        P(("own", "red"), None, None),
        P("own", "red", None, None, None),
        P("own", "red", None),
        P("own", "red", None),
        P("own", "red"),
    )
    return jax.shard_map(
        functools.partial(body, mesh.shape["own"], mesh.shape["red"]),
        mesh=mesh,
        in_specs=placed,
        out_specs=P(("own", "red"), None, None),
        check_vma=False,
    )
```

```python
import functools

import jax
import jax.numpy as jnp
from jax import lax
from jax.experimental import pallas as pl
from jax.experimental.pallas import tpu as pltpu
from jax.sharding import PartitionSpec as P

MESH = pl.DeviceIdType.MESH
CORES = 2
EARLY_PARTS = 2
GROUP = 4
ITEMS = 8


def flip_bits(value, mask):
    bit = 1
    while bit <= mask:
        if mask & bit:
            value = value + (1 - 2 * ((value // bit) % 2)) * bit
        bit *= 2
    return value


def product(amp_list, int_list):
    left = jnp.concatenate(amp_list, axis=1)
    right = jnp.concatenate(int_list, axis=0)
    return jnp.dot(left, right, preferred_element_type=jnp.float32)


def exchange_kernel(
    n_own, n_red, cap, rows, slots,
    req_hbm, amp_hbm, int_hbm, amp_at_hbm, int_at_hbm, count_hbm,
    amp_out, far_int, part, late,
    recv_amp, near_int, req_ref, tri_amp, tri_int, counts, amp_vec, int_vec, asked_vmem, asked_smem, amp_store, int_store, send_amp, send_int,
    req_send, req_recv, local_sem, tile_send, tile_recv,
):
    store = amp_store.shape[0]
    received = n_own * cap
    half_own = n_own // 2
    half_slots = half_own * cap
    me = lax.axis_index("own")
    my_half = me // half_own

    load_amp = pltpu.make_async_copy(amp_hbm, amp_store, local_sem.at[0])
    load_int = pltpu.make_async_copy(int_hbm, int_store, local_sem.at[1])
    load_req = pltpu.make_async_copy(req_hbm, req_ref, local_sem.at[3])
    load_req.start()
    load_amp.start()
    load_int.start()
    loads = []
    for index, (src, dst) in enumerate([
        (amp_at_hbm, tri_amp), (int_at_hbm, tri_int), (count_hbm, counts),
        (amp_at_hbm, amp_vec), (int_at_hbm, int_vec),
    ]):
        load = pltpu.make_async_copy(src, dst, local_sem.at[4 + index])
        load.start()
        loads.append(load)

    barrier = pltpu.get_barrier_semaphore()
    for step in range(1, n_own):
        pl.semaphore_signal(
            barrier, inc=1, device_id={"own": flip_bits(me, step)}, device_id_type=MESH
        )
    pl.semaphore_wait(barrier, n_own - 1)

    load_req.wait()
    asks = []
    for step in range(n_own - 1, 0, -1):
        peer = flip_bits(me, step)
        copy = pltpu.make_async_remote_copy(
            src_ref=req_ref.at[peer],
            dst_ref=asked_vmem.at[me],
            send_sem=req_send.at[step],
            recv_sem=req_recv.at[step],
            device_id={"own": peer},
            device_id_type=MESH,
        )
        copy.start()
        asks.append(copy)
    asked_vmem[me] = req_ref[me]
    for copy in asks:
        copy.wait()
    to_smem = pltpu.make_async_copy(asked_vmem, asked_smem, local_sem.at[2])
    to_smem.start()
    to_smem.wait()

    far = list(range(n_own - 1, half_own - 1, -1))
    near = list(range(half_own - 1, 0, -1))
    order = []
    for index, step in enumerate(far):
        order.append((0, step))
        if index < len(near):
            order.append((0, near[index]))
    for index, step in enumerate(far):
        if index < len(near):
            order.append((1, near[index]))
        order.append((1, step))

    def pack(kind, step, slot):
        peer = flip_bits(me, step)
        number = asked_smem[peer, kind, slot]
        source = (amp_store, int_store)[kind]
        tile = source[jnp.clip(number, 0, store - 1)]
        return tile.T if kind == 1 else tile

    my_place = (me % half_own) * cap
    recv_amp[received] = jnp.zeros_like(recv_amp[received])
    loaded = [False, False]
    copies = {}
    for kind, step in order:
        if not loaded[kind]:
            (load_amp, load_int)[kind].wait()
            loaded[kind] = True
        outbox = (send_amp, send_int)[kind]
        for slot in range(cap):
            outbox[step, slot] = pack(kind, step, slot)
        if kind == 0:
            inbox = recv_amp.at[pl.ds(me * cap, cap)]
        elif step >= half_own:
            inbox = far_int.at[pl.ds(my_place, cap)]
        else:
            inbox = near_int.at[pl.ds(my_place, cap)]
        copy = pltpu.make_async_remote_copy(
            src_ref=outbox.at[step],
            dst_ref=inbox,
            send_sem=tile_send.at[kind, step],
            recv_sem=tile_recv.at[kind, step],
            device_id={"own": flip_bits(me, step)},
            device_id_type=MESH,
        )
        copy.start()
        copies[kind, step] = copy
    for slot in range(cap):
        recv_amp[me * cap + slot] = pack(0, 0, slot)
        near_int[my_place + slot] = pack(1, 0, slot)

    for load in loads:
        load.wait()

    wide = late.shape[-1]
    row_at = lax.broadcasted_iota(jnp.int32, (rows, slots), 0)
    slot_at = lax.broadcasted_iota(jnp.int32, (rows, slots), 1)
    live = jnp.zeros((rows, slots), jnp.int32)
    for row in range(rows):
        live = jnp.where(row_at == row, counts[row], live)
    amp_at = amp_vec[:, 0, :]
    int_at = int_vec[:, 0, :]
    is_late = (slot_at < live) & ((int_at // half_slots) != my_half)
    late_one = jnp.where(is_late, 1.0, 0.0).astype(jnp.float32)
    before = jnp.where(
        lax.broadcasted_iota(jnp.int32, (slots, slots), 0)
        < lax.broadcasted_iota(jnp.int32, (slots, slots), 1),
        1.0, 0.0,
    ).astype(jnp.float32)
    rank = jnp.dot(late_one, before, preferred_element_type=jnp.float32).astype(jnp.int32)
    rank = jnp.where(is_late, rank, wide)
    place = lax.broadcasted_iota(jnp.int32, (rows, wide), 1)
    total = jnp.sum(late_one, axis=1, keepdims=True).astype(jnp.int32)
    amp_list = jnp.where(place == slots, total, received)
    int_list = jnp.zeros((rows, wide), jnp.int32)
    int_far = int_at % half_slots
    for k in range(slots):
        here = place == rank[:, k : k + 1]
        amp_list = jnp.where(here, amp_at[:, k : k + 1], amp_list)
        int_list = jnp.where(here, int_far[:, k : k + 1], int_list)
    late[0] = amp_list
    late[1] = int_list

    blocks = (total + (GROUP - 1)) // GROUP
    group_at = lax.broadcasted_iota(jnp.int32, (rows, 1), 0) // (rows // n_red)
    blocks = jnp.where(group_at == lax.axis_index("red"), 0, blocks).astype(jnp.float32)
    lower = jnp.where(
        lax.broadcasted_iota(jnp.int32, (rows, rows), 1)
        < lax.broadcasted_iota(jnp.int32, (rows, rows), 0),
        1.0, 0.0,
    ).astype(jnp.float32)
    ahead = jnp.dot(
        lower, jnp.broadcast_to(blocks, (rows, wide)), preferred_element_type=jnp.float32
    ).astype(jnp.int32)
    item_count = jnp.sum(blocks).astype(jnp.int32)
    item_rows = rows * slots // GROUP // wide
    for line in range(item_rows):
        item = lax.broadcasted_iota(jnp.int32, (rows, wide), 1) + line * wide
        begun = ahead <= item
        row_of = jnp.sum(begun.astype(jnp.int32), axis=0, keepdims=True) - 1
        start = jnp.max(jnp.where(begun, ahead, 0), axis=0, keepdims=True)
        first_of = (item[:1] - start) * GROUP
        listed = item[:1] < item_count
        late[2, line : line + 1] = jnp.where(listed, row_of, 0)
        late[2, item_rows + line : item_rows + line + 1] = jnp.where(
            listed, first_of, slots + GROUP
        )
    late[2, 2 * item_rows : 2 * item_rows + 1] = jnp.broadcast_to(item_count, (1, wide))

    for kind, step in order:
        if kind == 0 or step < half_own:
            copies[kind, step].wait_recv()
    keep_amp = pltpu.make_async_copy(recv_amp, amp_out, local_sem.at[9])
    keep_amp.start()

    def one_row(row, carry):
        count = counts[row]
        total = None
        for piece in range(EARLY_PARTS):
            amps, ints = [], []
            for k in range(slots // EARLY_PARTS):
                slot = piece * (slots // EARLY_PARTS) + k
                at = tri_int[row, 0, slot]
                early = ((at // half_slots) == my_half) & (slot < count)
                amps.append(recv_amp[jnp.where(early, tri_amp[row, 0, slot], received)])
                ints.append(near_int[at % half_slots])
            value = product(amps, ints)
            total = value if total is None else total + value
        part[row] = total
        return carry

    lax.fori_loop(0, rows, one_row, 0)

    for kind, step in order:
        if kind == 1 and step >= half_own:
            copies[kind, step].wait_recv()
    for kind, step in order:
        copies[kind, step].wait_send()
    keep_amp.wait()


def late_kernel(rows, slots, late, recv_amp, far_int, part, out):
    wide = late.shape[-1]
    item_rows = rows * slots // GROUP // wide

    def some(block, carry):
        found = []
        for index in range(ITEMS):
            item = block * ITEMS + index
            line, column = item // wide, item % wide
            row = late[2, line, column]
            first = late[2, item_rows + line, column]
            amps = [recv_amp[late[0, row, first + k]] for k in range(GROUP)]
            ints = [far_int[late[1, row, first + k]] for k in range(GROUP)]
            found.append((row, product(amps, ints)))
        for row, value in found:
            out[row] += value
        return carry

    items = late[2, 2 * item_rows, 0]
    lax.fori_loop(0, (items + ITEMS - 1) // ITEMS, some, 0)


def scatter_kernel(
    n_red, slots, late, recv_amp, far_int, part,
    out_ref, listed, mid, sib, across, list_sem, sib_send, sib_recv, across_send, across_recv
):
    n_x = n_red // CORES
    per_dev = part.shape[0] // n_red
    red = lax.axis_index("red")
    my_x, my_core = red // CORES, red % CORES
    sibling = my_x * CORES + (1 - my_core)
    load_list = pltpu.make_async_copy(late.at[pl.ds(0, 2)], listed, list_sem)
    load_list.start()

    barrier = pltpu.get_barrier_semaphore()
    pl.semaphore_signal(barrier, inc=1, device_id={"red": sibling}, device_id_type=MESH)
    for step in range(1, n_x):
        peer = ((my_x + step) % n_x) * CORES + my_core
        pl.semaphore_signal(barrier, inc=1, device_id={"red": peer}, device_id_type=MESH)
    pl.semaphore_wait(barrier, n_x)

    def to_sibling(step, j):
        x = (my_x + step) % n_x
        return pltpu.make_async_remote_copy(
            src_ref=part.at[(x * CORES + (1 - my_core)) * per_dev + j],
            dst_ref=sib.at[step, j],
            send_sem=sib_send.at[step, j],
            recv_sem=sib_recv.at[step, j],
            device_id={"red": sibling},
            device_id_type=MESH,
        )

    def to_across(step, j):
        x = (my_x + step) % n_x
        return pltpu.make_async_remote_copy(
            src_ref=mid.at[step - 1, j],
            dst_ref=across.at[step - 1, j],
            send_sem=across_send.at[step - 1, j],
            recv_sem=across_recv.at[step - 1, j],
            device_id={"red": x * CORES + my_core},
            device_id_type=MESH,
        )

    order = list(range(1, n_x)) + [0]
    for step in order:
        for j in range(per_dev):
            to_sibling(step, j).start()
    for step in range(1, n_x):
        x = (my_x + step) % n_x
        for j in range(per_dev):
            to_sibling(step, j).wait_recv()
            row = (x * CORES + my_core) * per_dev + j
            mid[step - 1, j] = part[row] + sib[step, j]
            to_across(step, j).start()

    load_list.wait()

    def own_row(j, carry):
        row = red * per_dev + j
        total = part[row]
        for piece in range(EARLY_PARTS):
            share = slots // EARLY_PARTS
            places = range(piece * share, (piece + 1) * share)
            amps = [recv_amp[listed[0, row, k]] for k in places]
            ints = [far_int[listed[1, row, k]] for k in places]
            total = total + product(amps, ints)
        out_ref[j] = total
        return carry

    lax.fori_loop(0, per_dev, own_row, 0)
    for j in range(per_dev):
        to_sibling(0, j).wait_recv()
        out_ref[j] += sib[0, j]
    for step in range(1, n_x):
        for j in range(per_dev):
            to_across(step, j).wait_recv()
            out_ref[j] += across[step - 1, j]
    for step in order:
        for j in range(per_dev):
            to_sibling(step, j).wait_send()
            if step:
                to_across(step, j).wait_send()


def body(n_own, n_red, amp_tiles, int_tiles, requests, tri_amp, tri_int, tri_count):
    rows, _, slots = tri_amp.shape
    cap = requests.shape[-1]
    tile = amp_tiles.shape[1:]
    store = amp_tiles.shape[0]
    received = n_own * cap
    n_x = n_red // CORES
    per_dev = rows // n_red
    kind = amp_tiles.dtype
    vmem = pl.BlockSpec(memory_space=pltpu.VMEM)
    smem = pl.BlockSpec(memory_space=pltpu.SMEM)
    hbm = pl.BlockSpec(memory_space=pltpu.HBM)
    dma = pltpu.SemaphoreType.DMA
    shape = jax.ShapeDtypeStruct
    partial = shape((rows,) + tile, jnp.float32)
    counts = tri_count.reshape(rows)
    recv_amp, far_int, early, late = pl.pallas_call(
        functools.partial(exchange_kernel, n_own, n_red, cap, rows, slots),
        out_shape=[
            shape((received + 1,) + tile, kind),
            shape((received // 2,) + tile, kind),
            partial,
            shape((3, rows, 2 * slots), jnp.int32),
        ],
        in_specs=[hbm] * 6,
        out_specs=[hbm, vmem, vmem, vmem],
        scratch_shapes=[
            pltpu.VMEM((received + 1,) + tile, kind),
            pltpu.VMEM((received // 2,) + tile, kind),
            pltpu.VMEM((n_own, 2, cap), jnp.int32),
            pltpu.SMEM((rows, 1, slots), jnp.int32),
            pltpu.SMEM((rows, 1, slots), jnp.int32),
            pltpu.SMEM((rows,), jnp.int32),
            pltpu.VMEM((rows, 1, slots), jnp.int32),
            pltpu.VMEM((rows, 1, slots), jnp.int32),
            pltpu.VMEM((n_own, 2, cap), jnp.int32),
            pltpu.SMEM((n_own, 2, cap), jnp.int32),
            pltpu.VMEM((store,) + tile, kind),
            pltpu.VMEM((store,) + tile, kind),
            pltpu.VMEM((n_own, cap) + tile, kind),
            pltpu.VMEM((n_own, cap) + tile, kind),
            dma((n_own,)),
            dma((n_own,)),
            dma((10,)),
            dma((2, n_own)),
            dma((2, n_own)),
        ],
        compiler_params=pltpu.CompilerParams(
            collective_id=0, has_side_effects=True, vmem_limit_bytes=50 * 2**20
        ),
    )(requests[0, 0], amp_tiles, int_tiles, tri_amp, tri_int, counts)
    summed = pl.pallas_call(
        functools.partial(late_kernel, rows, slots),
        out_shape=partial,
        in_specs=[smem, vmem, vmem, vmem],
        out_specs=vmem,
        input_output_aliases={3: 0},
        compiler_params=pltpu.CompilerParams(vmem_limit_bytes=32 * 2**20),
    )(late, recv_amp, far_int, early)
    return pl.pallas_call(
        functools.partial(scatter_kernel, n_red, slots),
        out_shape=shape((per_dev,) + tile, jnp.float32),
        in_specs=[vmem] * 4,
        out_specs=vmem,
        scratch_shapes=[
            pltpu.SMEM((2, rows, 2 * slots), jnp.int32),
            pltpu.VMEM((n_x - 1, per_dev) + tile, jnp.float32),
            pltpu.VMEM((n_x, per_dev) + tile, jnp.float32),
            pltpu.VMEM((n_x - 1, per_dev) + tile, jnp.float32),
            dma,
            dma((n_x, per_dev)),
            dma((n_x, per_dev)),
            dma((n_x - 1, per_dev)),
            dma((n_x - 1, per_dev)),
        ],
        compiler_params=pltpu.CompilerParams(
            collective_id=1, has_side_effects=True, vmem_limit_bytes=32 * 2**20
        ),
    )(late, recv_amp, far_int, summed)


def solution(mesh):
    placed = (
        P(("own", "red"), None, None),
        P(("own", "red"), None, None),
        P("own", "red", None, None, None),
        P("own", "red", None),
        P("own", "red", None),
        P("own", "red"),
    )
    return jax.shard_map(
        functools.partial(body, mesh.shape["own"], mesh.shape["red"]),
        mesh=mesh,
        in_specs=placed,
        out_specs=P(("own", "red"), None, None),
        check_vma=False,
    )
```

```python
import functools

import jax
import jax.numpy as jnp
from jax import lax
from jax.experimental import pallas as pl
from jax.experimental.pallas import tpu as pltpu
from jax.sharding import PartitionSpec as P

MESH = pl.DeviceIdType.MESH
CORES = 2
EARLY_PARTS = 2
GROUP = 4
ITEMS = 8


def flip_bits(value, mask):
    bit = 1
    while bit <= mask:
        if mask & bit:
            value = value + (1 - 2 * ((value // bit) % 2)) * bit
        bit *= 2
    return value


def product(amp_list, int_list):
    left = jnp.concatenate(amp_list, axis=1)
    right = jnp.concatenate(int_list, axis=0)
    return jnp.dot(left, right, preferred_element_type=jnp.float32)


def exchange_kernel(
    n_own, n_red, cap, rows, slots,
    req_hbm, amp_hbm, int_hbm, amp_at_hbm, int_at_hbm, count_hbm,
    amp_out, far_int, part, late,
    recv_amp, near_int, req_ref, tri_amp, tri_int, counts, amp_vec, int_vec, asked_vmem, asked_smem, amp_store, int_store, send_amp, send_int,
    req_send, req_recv, local_sem, list_sem, tile_send, tile_recv,
):
    store = amp_store.shape[0]
    received = n_own * cap
    half_own = n_own // 2
    half_slots = half_own * cap
    me = lax.axis_index("own")
    my_half = me // half_own

    load_amp = pltpu.make_async_copy(amp_hbm, amp_store, local_sem.at[0])
    load_int = pltpu.make_async_copy(int_hbm, int_store, local_sem.at[1])
    load_req = pltpu.make_async_copy(req_hbm, req_ref, local_sem.at[3])
    load_req.start()
    load_amp.start()
    load_int.start()
    loads = []
    for index, (src, dst) in enumerate([
        (amp_at_hbm, tri_amp), (int_at_hbm, tri_int), (count_hbm, counts),
        (amp_at_hbm, amp_vec), (int_at_hbm, int_vec),
    ]):
        load = pltpu.make_async_copy(src, dst, local_sem.at[4 + index])
        load.start()
        loads.append(load)

    barrier = pltpu.get_barrier_semaphore()
    for step in range(1, n_own):
        pl.semaphore_signal(
            barrier, inc=1, device_id={"own": flip_bits(me, step)}, device_id_type=MESH
        )
    pl.semaphore_wait(barrier, n_own - 1)

    load_req.wait()
    asks = []
    for step in range(n_own - 1, 0, -1):
        peer = flip_bits(me, step)
        copy = pltpu.make_async_remote_copy(
            src_ref=req_ref.at[peer],
            dst_ref=asked_vmem.at[me],
            send_sem=req_send.at[step],
            recv_sem=req_recv.at[step],
            device_id={"own": peer},
            device_id_type=MESH,
        )
        copy.start()
        asks.append(copy)
    asked_vmem[me] = req_ref[me]
    asks = dict(zip(range(n_own - 1, 0, -1), asks))

    def read_ask(step):
        if step:
            asks[step].wait_recv()
        row = pl.ds(flip_bits(me, step), 1)
        to_smem = pltpu.make_async_copy(
            asked_vmem.at[row], asked_smem.at[row], list_sem.at[step]
        )
        to_smem.start()
        to_smem.wait()

    far = list(range(n_own - 1, half_own - 1, -1))
    near = list(range(half_own - 1, 0, -1))
    order = []
    for index, step in enumerate(far):
        order.append((0, step))
        if index < len(near):
            order.append((0, near[index]))
    for index, step in enumerate(far):
        if index < len(near):
            order.append((1, near[index]))
        order.append((1, step))

    def pack(kind, step, slot):
        peer = flip_bits(me, step)
        number = asked_smem[peer, kind, slot]
        source = (amp_store, int_store)[kind]
        tile = source[jnp.clip(number, 0, store - 1)]
        return tile.T if kind == 1 else tile

    my_place = (me % half_own) * cap
    recv_amp[received] = jnp.zeros_like(recv_amp[received])
    loaded = [False, False]
    copies = {}
    for kind, step in order:
        if not loaded[kind]:
            (load_amp, load_int)[kind].wait()
            loaded[kind] = True
        outbox = (send_amp, send_int)[kind]
        if kind == 0:
            read_ask(step)
        for slot in range(cap):
            outbox[step, slot] = pack(kind, step, slot)
        if kind == 0:
            inbox = recv_amp.at[pl.ds(me * cap, cap)]
        elif step >= half_own:
            inbox = far_int.at[pl.ds(my_place, cap)]
        else:
            inbox = near_int.at[pl.ds(my_place, cap)]
        copy = pltpu.make_async_remote_copy(
            src_ref=outbox.at[step],
            dst_ref=inbox,
            send_sem=tile_send.at[kind, step],
            recv_sem=tile_recv.at[kind, step],
            device_id={"own": flip_bits(me, step)},
            device_id_type=MESH,
        )
        copy.start()
        copies[kind, step] = copy
    read_ask(0)
    for slot in range(cap):
        recv_amp[me * cap + slot] = pack(0, 0, slot)
        near_int[my_place + slot] = pack(1, 0, slot)

    for load in loads:
        load.wait()

    wide = late.shape[-1]
    row_at = lax.broadcasted_iota(jnp.int32, (rows, slots), 0)
    slot_at = lax.broadcasted_iota(jnp.int32, (rows, slots), 1)
    live = jnp.zeros((rows, slots), jnp.int32)
    for row in range(rows):
        live = jnp.where(row_at == row, counts[row], live)
    amp_at = amp_vec[:, 0, :]
    int_at = int_vec[:, 0, :]
    is_late = (slot_at < live) & ((int_at // half_slots) != my_half)
    late_one = jnp.where(is_late, 1.0, 0.0).astype(jnp.float32)
    before = jnp.where(
        lax.broadcasted_iota(jnp.int32, (slots, slots), 0)
        < lax.broadcasted_iota(jnp.int32, (slots, slots), 1),
        1.0, 0.0,
    ).astype(jnp.float32)
    rank = jnp.dot(late_one, before, preferred_element_type=jnp.float32).astype(jnp.int32)
    rank = jnp.where(is_late, rank, wide)
    place = lax.broadcasted_iota(jnp.int32, (rows, wide), 1)
    total = jnp.sum(late_one, axis=1, keepdims=True).astype(jnp.int32)
    amp_list = jnp.where(place == slots, total, received)
    int_list = jnp.zeros((rows, wide), jnp.int32)
    int_far = int_at % half_slots
    for k in range(slots):
        here = place == rank[:, k : k + 1]
        amp_list = jnp.where(here, amp_at[:, k : k + 1], amp_list)
        int_list = jnp.where(here, int_far[:, k : k + 1], int_list)
    late[0] = amp_list
    late[1] = int_list

    blocks = (total + (GROUP - 1)) // GROUP
    group_at = lax.broadcasted_iota(jnp.int32, (rows, 1), 0) // (rows // n_red)
    blocks = jnp.where(group_at == lax.axis_index("red"), 0, blocks).astype(jnp.float32)
    lower = jnp.where(
        lax.broadcasted_iota(jnp.int32, (rows, rows), 1)
        < lax.broadcasted_iota(jnp.int32, (rows, rows), 0),
        1.0, 0.0,
    ).astype(jnp.float32)
    ahead = jnp.dot(
        lower, jnp.broadcast_to(blocks, (rows, wide)), preferred_element_type=jnp.float32
    ).astype(jnp.int32)
    item_count = jnp.sum(blocks).astype(jnp.int32)
    item_rows = rows * slots // GROUP // wide
    for line in range(item_rows):
        item = lax.broadcasted_iota(jnp.int32, (rows, wide), 1) + line * wide
        begun = ahead <= item
        row_of = jnp.sum(begun.astype(jnp.int32), axis=0, keepdims=True) - 1
        start = jnp.max(jnp.where(begun, ahead, 0), axis=0, keepdims=True)
        first_of = (item[:1] - start) * GROUP
        listed = item[:1] < item_count
        late[2, line : line + 1] = jnp.where(listed, row_of, 0)
        late[2, item_rows + line : item_rows + line + 1] = jnp.where(
            listed, first_of, slots + GROUP
        )
    late[2, 2 * item_rows : 2 * item_rows + 1] = jnp.broadcast_to(item_count, (1, wide))

    for kind, step in order:
        if kind == 0 or step < half_own:
            copies[kind, step].wait_recv()
    keep_amp = pltpu.make_async_copy(recv_amp, amp_out, local_sem.at[9])
    keep_amp.start()

    def one_row(row, carry):
        count = counts[row]
        total = None
        for piece in range(EARLY_PARTS):
            amps, ints = [], []
            for k in range(slots // EARLY_PARTS):
                slot = piece * (slots // EARLY_PARTS) + k
                at = tri_int[row, 0, slot]
                early = ((at // half_slots) == my_half) & (slot < count)
                amps.append(recv_amp[jnp.where(early, tri_amp[row, 0, slot], received)])
                ints.append(near_int[at % half_slots])
            value = product(amps, ints)
            total = value if total is None else total + value
        part[row] = total
        return carry

    lax.fori_loop(0, rows, one_row, 0)

    for kind, step in order:
        if kind == 1 and step >= half_own:
            copies[kind, step].wait_recv()
    for kind, step in order:
        copies[kind, step].wait_send()
        if kind == 0:
            asks[step].wait_send()
    keep_amp.wait()


def late_kernel(rows, slots, late, amp_hbm, far_int, part, out, recv_amp, amp_sem):
    load_amp = pltpu.make_async_copy(amp_hbm, recv_amp, amp_sem)
    load_amp.start()
    wide = late.shape[-1]
    item_rows = rows * slots // GROUP // wide

    def some(block, carry):
        found = []
        for index in range(ITEMS):
            item = block * ITEMS + index
            line, column = item // wide, item % wide
            row = late[2, line, column]
            first = late[2, item_rows + line, column]
            amps = [recv_amp[late[0, row, first + k]] for k in range(GROUP)]
            ints = [far_int[late[1, row, first + k]] for k in range(GROUP)]
            found.append((row, product(amps, ints)))
        for row, value in found:
            out[row] += value
        return carry

    items = late[2, 2 * item_rows, 0]
    load_amp.wait()
    lax.fori_loop(0, (items + ITEMS - 1) // ITEMS, some, 0)


def scatter_kernel(
    n_red, slots, late, amp_hbm, far_int, part,
    out_ref, recv_amp, listed, mid, sib, across, list_sem, amp_sem, sib_send, sib_recv, across_send, across_recv
):
    n_x = n_red // CORES
    per_dev = part.shape[0] // n_red
    red = lax.axis_index("red")
    my_x, my_core = red // CORES, red % CORES
    sibling = my_x * CORES + (1 - my_core)
    load_list = pltpu.make_async_copy(late.at[pl.ds(0, 2)], listed, list_sem)
    load_list.start()
    load_amp = pltpu.make_async_copy(amp_hbm, recv_amp, amp_sem)
    load_amp.start()

    barrier = pltpu.get_barrier_semaphore()
    pl.semaphore_signal(barrier, inc=1, device_id={"red": sibling}, device_id_type=MESH)
    for step in range(1, n_x):
        peer = ((my_x + step) % n_x) * CORES + my_core
        pl.semaphore_signal(barrier, inc=1, device_id={"red": peer}, device_id_type=MESH)
    pl.semaphore_wait(barrier, n_x)

    def to_sibling(step, j):
        x = (my_x + step) % n_x
        return pltpu.make_async_remote_copy(
            src_ref=part.at[(x * CORES + (1 - my_core)) * per_dev + j],
            dst_ref=sib.at[step, j],
            send_sem=sib_send.at[step, j],
            recv_sem=sib_recv.at[step, j],
            device_id={"red": sibling},
            device_id_type=MESH,
        )

    def to_across(step, j):
        x = (my_x + step) % n_x
        return pltpu.make_async_remote_copy(
            src_ref=mid.at[step - 1, j],
            dst_ref=across.at[step - 1, j],
            send_sem=across_send.at[step - 1, j],
            recv_sem=across_recv.at[step - 1, j],
            device_id={"red": x * CORES + my_core},
            device_id_type=MESH,
        )

    order = list(range(1, n_x)) + [0]
    for step in order:
        for j in range(per_dev):
            to_sibling(step, j).start()
    for step in range(1, n_x):
        x = (my_x + step) % n_x
        for j in range(per_dev):
            to_sibling(step, j).wait_recv()
            row = (x * CORES + my_core) * per_dev + j
            mid[step - 1, j] = part[row] + sib[step, j]
            to_across(step, j).start()

    load_list.wait()
    load_amp.wait()

    def own_row(j, carry):
        row = red * per_dev + j
        total = part[row]
        for piece in range(EARLY_PARTS):
            share = slots // EARLY_PARTS
            places = range(piece * share, (piece + 1) * share)
            amps = [recv_amp[listed[0, row, k]] for k in places]
            ints = [far_int[listed[1, row, k]] for k in places]
            total = total + product(amps, ints)
        out_ref[j] = total
        return carry

    lax.fori_loop(0, per_dev, own_row, 0)
    for j in range(per_dev):
        to_sibling(0, j).wait_recv()
        out_ref[j] += sib[0, j]
    for step in range(1, n_x):
        for j in range(per_dev):
            to_across(step, j).wait_recv()
            out_ref[j] += across[step - 1, j]
    for step in order:
        for j in range(per_dev):
            to_sibling(step, j).wait_send()
            if step:
                to_across(step, j).wait_send()


def body(n_own, n_red, amp_tiles, int_tiles, requests, tri_amp, tri_int, tri_count):
    rows, _, slots = tri_amp.shape
    cap = requests.shape[-1]
    tile = amp_tiles.shape[1:]
    store = amp_tiles.shape[0]
    received = n_own * cap
    n_x = n_red // CORES
    per_dev = rows // n_red
    kind = amp_tiles.dtype
    vmem = pl.BlockSpec(memory_space=pltpu.VMEM)
    smem = pl.BlockSpec(memory_space=pltpu.SMEM)
    hbm = pl.BlockSpec(memory_space=pltpu.HBM)
    dma = pltpu.SemaphoreType.DMA
    shape = jax.ShapeDtypeStruct
    partial = shape((rows,) + tile, jnp.float32)
    counts = tri_count.reshape(rows)
    recv_amp, far_int, early, late = pl.pallas_call(
        functools.partial(exchange_kernel, n_own, n_red, cap, rows, slots),
        out_shape=[
            shape((received + 1,) + tile, kind),
            shape((received // 2,) + tile, kind),
            partial,
            shape((3, rows, 2 * slots), jnp.int32),
        ],
        in_specs=[hbm] * 6,
        out_specs=[hbm, vmem, vmem, vmem],
        scratch_shapes=[
            pltpu.VMEM((received + 1,) + tile, kind),
            pltpu.VMEM((received // 2,) + tile, kind),
            pltpu.VMEM((n_own, 2, cap), jnp.int32),
            pltpu.SMEM((rows, 1, slots), jnp.int32),
            pltpu.SMEM((rows, 1, slots), jnp.int32),
            pltpu.SMEM((rows,), jnp.int32),
            pltpu.VMEM((rows, 1, slots), jnp.int32),
            pltpu.VMEM((rows, 1, slots), jnp.int32),
            pltpu.VMEM((n_own, 2, cap), jnp.int32),
            pltpu.SMEM((n_own, 2, cap), jnp.int32),
            pltpu.VMEM((store,) + tile, kind),
            pltpu.VMEM((store,) + tile, kind),
            pltpu.VMEM((n_own, cap) + tile, kind),
            pltpu.VMEM((n_own, cap) + tile, kind),
            dma((n_own,)),
            dma((n_own,)),
            dma((10,)),
            dma((n_own,)),
            dma((2, n_own)),
            dma((2, n_own)),
        ],
        compiler_params=pltpu.CompilerParams(
            collective_id=0, has_side_effects=True, vmem_limit_bytes=50 * 2**20
        ),
    )(requests[0, 0], amp_tiles, int_tiles, tri_amp, tri_int, counts)
    summed = pl.pallas_call(
        functools.partial(late_kernel, rows, slots),
        out_shape=partial,
        in_specs=[smem, hbm, vmem, vmem],
        out_specs=vmem,
        scratch_shapes=[pltpu.VMEM((received + 1,) + tile, kind), dma],
        input_output_aliases={3: 0},
        compiler_params=pltpu.CompilerParams(vmem_limit_bytes=50 * 2**20),
    )(late, recv_amp, far_int, early)
    return pl.pallas_call(
        functools.partial(scatter_kernel, n_red, slots),
        out_shape=shape((per_dev,) + tile, jnp.float32),
        in_specs=[vmem, hbm, vmem, vmem],
        out_specs=vmem,
        scratch_shapes=[
            pltpu.VMEM((received + 1,) + tile, kind),
            pltpu.SMEM((2, rows, 2 * slots), jnp.int32),
            pltpu.VMEM((n_x - 1, per_dev) + tile, jnp.float32),
            pltpu.VMEM((n_x, per_dev) + tile, jnp.float32),
            pltpu.VMEM((n_x - 1, per_dev) + tile, jnp.float32),
            dma,
            dma,
            dma((n_x, per_dev)),
            dma((n_x, per_dev)),
            dma((n_x - 1, per_dev)),
            dma((n_x - 1, per_dev)),
        ],
        compiler_params=pltpu.CompilerParams(
            collective_id=1, has_side_effects=True, vmem_limit_bytes=50 * 2**20
        ),
    )(late, recv_amp, far_int, summed)


def solution(mesh):
    placed = (
        P(("own", "red"), None, None),
        P(("own", "red"), None, None),
        P("own", "red", None, None, None),
        P("own", "red", None),
        P("own", "red", None),
        P("own", "red"),
    )
    return jax.shard_map(
        functools.partial(body, mesh.shape["own"], mesh.shape["red"]),
        mesh=mesh,
        in_specs=placed,
        out_specs=P(("own", "red"), None, None),
        check_vma=False,
    )
```
